32 devices in a mesh: dp: 16 (over z, y, x), mp: 2 (over core).
Axes of the slice: x: 2, y: 2, z: 4, core: 2. Of those that a mesh axis runs over, the one named last changes fastest.
Arguments:
- store_rows: bfloat16 [4096, 8192], P('dp', 'mp'), may hold values from -6 to 6
- source_shard: int32 [512], replicated, may hold values from 0 to 15, as said below
- source_row: int32 [512], replicated, may hold values from 0 to 255
- state_len: int32 [16], replicated, may hold values from 1 to 64, 512 in all
- visits: int32 [16], replicated, may hold values from 1 to 4095
- gain: bfloat16 [8192], P('mp'), may hold values from 0.5 to 1.5
- w_gate: bfloat16 [8192, 22016], P('mp', 'dp'), may hold values from -0.0625 to 0.0625
- w_up: bfloat16 [8192, 22016], P('mp', 'dp'), may hold values from -0.0625 to 0.0625
- w_down: bfloat16 [22016, 8192], P('dp', 'mp'), may hold values from -0.0390625 to 0.0390625
- upstream: bfloat16 [512, 8192], P(None, 'mp'), may hold values from -0.52734375 to 0.52734375
Outputs:
- layer_out: bfloat16 [512, 8192], P('dp', 'mp')
- grad_gate: bfloat16 [8192, 22016], P('mp', 'dp')
- grad_up: bfloat16 [8192, 22016], P('mp', 'dp')
- grad_down: bfloat16 [22016, 8192], P('dp', 'mp')
The draws below stay inside these ranges and needn't reach their ends.
Inputs may be any that keep to these rules, and one draw needn't show every extreme that they name: `source_shard`: block b holds training rows b * 32 to (b + 1) * 32 - 1. No shard is named more than 4 times in one block nor more than 64 times in all; one shard, drawn from the seed, is named exactly 4 times in every block. `state_len`: the lengths sum to 512.
All inputs are finite; a program needn't handle non-finite values.
Results may differ from the reference program's by a relative error of at most 0.017.
Values may be sent and summed in bfloat16 or wider, within the bound.
A program may use at most 192 MiB of HBM per device.

```python
import math
import jax
import jax.numpy as jnp
import numpy as np
from jax import lax

D = 8192
FF = 22016
ROW_DP = 32
STORE_DEV = 256
ROWS = 512
STORE = 4096
STATES = 16
LEN_MAX = 64
PAIR_CAP = 4
N_DP = 16


def draw_source_shard(key, part):
    key_hot = jax.random.fold_in(key, 11)
    key_order = jax.random.fold_in(key, 12)
    key_place = jax.random.fold_in(key, 13)
    hot_shard = jax.random.randint(key_hot, (), 0, N_DP).astype(jnp.int32)
    others = ((hot_shard + 1 + jax.random.permutation(key_order, N_DP - 1).astype(jnp.int32)) % N_DP).astype(jnp.int32)
    homes = jnp.arange(N_DP, dtype=jnp.int32)
    place_keys = jax.vmap(lambda home: jax.random.fold_in(key_place, home))(homes)
    places = jax.vmap(lambda one_key: jax.random.permutation(one_key, ROW_DP))(place_keys).astype(jnp.int32)
    cold_count = ROW_DP - PAIR_CAP
    cold_slot = ((places - PAIR_CAP + homes[:, None] * cold_count) % (N_DP - 1)).astype(jnp.int32)
    source = jnp.where(places < PAIR_CAP, hot_shard, others[cold_slot])
    return source.reshape(-1).astype(jnp.int32)


def with_ends(drawn, rng, low, high):
    shape = drawn.shape
    index_at = [jax.random.randint(jax.random.fold_in(rng, axis), (), 0, shape[axis]) for axis in range(len(shape))]
    drawn = drawn.at[tuple(index_at)].set(low)
    longest = shape.index(max(shape))
    index_at[longest] = (index_at[longest] + 1) % shape[longest]
    return drawn.at[tuple(index_at)].set(high)


def steps_of(stream_key, dims, pieces, smallest, top_value):
    def one(dim, blocks):
        heights = jax.random.uniform(jax.random.fold_in(jax.random.fold_in(stream_key, 6), dim), (blocks,), jnp.float32, smallest / len(pieces), top_value / len(pieces))
        return jnp.repeat(jnp.exp(heights), dims[dim] // blocks).reshape((-1,) + (1,) * (len(dims) - dim - 1))

    factor_of = one(*pieces[0])
    for cut in pieces[1:]:
        factor_of = factor_of * one(*cut)
    return factor_of


def profile(amount, total, reach, lean):
    loads = [(1 << 20) // math.isqrt(grade ** lean) + 1 for grade in range(2, amount + 1)]
    spare, holding = total - reach - (amount - 1), [1] * (amount - 1)
    while spare > 0:
        movable = [i for i in range(amount - 1) if holding[i] < reach]
        mass, left = sum([loads[i] for i in movable]), spare
        for i in movable:
            more = min(reach - holding[i], max(1, left * loads[i] // mass), spare)
            holding[i] = holding[i] + more
            spare = spare - more
    return np.array([reach] + holding)


def uneven(own_key, amount, total, bound, slope):
    if amount == 2:
        one = jax.random.randint(own_key, (), max(1, total - bound), min(bound, total - 1) + 1)
        return jnp.stack([one, total - one])
    tallies = jnp.asarray(profile(amount, total, bound, slope), jnp.int32)
    pairs = (amount - 1) // 2
    donor, taker = tallies[1:1 + 2 * pairs:2], tallies[2:2 + 2 * pairs:2]
    room = jnp.minimum(donor - 1, bound - taker)
    passed = jax.random.randint(jax.random.fold_in(own_key, 1), (pairs,), 0, 1 << 20) % (room + 1)
    tallies = tallies.at[1:1 + 2 * pairs:2].set(donor - passed).at[2:2 + 2 * pairs:2].set(taker + passed)
    return tallies[jax.random.permutation(jax.random.fold_in(own_key, 2), amount)]


def centred(rng, dims, width, reach, pieces=(), held_as=jnp.bfloat16):
    entries = width * jax.random.normal(rng, dims, jnp.float32)
    if pieces:
        entries = entries * steps_of(rng, dims, pieces, -0.22, 0.18)
    return jnp.clip(entries, -reach, reach).astype(held_as)


def setup_inputs(seed: int = 0) -> dict:
    streams_of = jax.random.split(jax.random.key(seed), 11)
    return {
        "store_rows": centred(streams_of[0], (STORE, D), 1.0, 6.0, ((0, 16), (1, 2))),
        "source_shard": draw_source_shard(jax.random.fold_in(streams_of[10], 71), 0),
        "source_row": with_ends(jax.random.randint(streams_of[2], (ROWS,), 0, STORE_DEV), jax.random.fold_in(streams_of[2], 1), 0, STORE_DEV - 1).astype(jnp.int32),
        "state_len": uneven(streams_of[3], STATES, ROWS, LEN_MAX, 1).astype(jnp.int32),
        "visits": with_ends(jax.random.randint(streams_of[4], (STATES,), 1, 4096), jax.random.fold_in(streams_of[4], 1), 1, 4095).astype(jnp.int32),
        "gain": jnp.clip(1.0 + 0.1 * jax.random.normal(streams_of[5], (D,), jnp.float32), 0.5, 1.5).astype(jnp.bfloat16),
        "w_gate": centred(streams_of[6], (D, FF), D ** -0.5, 0.0625, ((0, 2), (1, 16))),
        "w_up": centred(streams_of[7], (D, FF), D ** -0.5, 0.0625, ((0, 2), (1, 16))),
        "w_down": centred(streams_of[8], (FF, D), FF ** -0.5, 0.0390625, ((0, 16), (1, 2))),
        "upstream": centred(streams_of[9], (ROWS, D), (2.0 / ROWS ** 0.5), 0.52734375, ((1, 2),)),
    }


epsilon = 1e-05

def reference(store_rows, source_shard, source_row, state_len, visits, gain, w_gate, w_up, w_down, upstream):
    index = (source_shard * STORE_DEV + source_row).astype(jnp.int32)
    train_rows = store_rows[index].astype(jnp.float32)
    squares = lax.optimization_barrier(jnp.sum(train_rows * train_rows, axis=1))
    inverse = lax.rsqrt(squares / D + epsilon)
    scaled = (train_rows * gain.astype(jnp.float32)[None, :]).astype(jnp.bfloat16)
    gate = inverse[:, None] * jnp.dot(scaled, w_gate, preferred_element_type=jnp.float32)
    up_all = inverse[:, None] * jnp.dot(scaled, w_up, preferred_element_type=jnp.float32)
    hidden = (jax.nn.silu(gate) * up_all).astype(jnp.bfloat16)
    layer_out = (train_rows + jnp.dot(hidden, w_down, preferred_element_type=jnp.float32)).astype(jnp.bfloat16)
    ends = jnp.cumsum(state_len).astype(jnp.int32)
    starts = (ends - state_len).astype(jnp.int32)
    row_ids = jnp.arange(ROWS, dtype=jnp.int32)
    member = ((row_ids[:, None] >= starts[None, :]) & (row_ids[:, None] < ends[None, :])).astype(jnp.float32)
    importance = jnp.log1p(visits.astype(jnp.float32))
    per_state = ROWS * importance / (state_len.astype(jnp.float32) * jnp.sum(importance))
    row_weight = lax.optimization_barrier(jnp.sum(member * per_state[None, :], axis=1))
    out_grad = (upstream.astype(jnp.float32) * row_weight[:, None]).astype(jnp.bfloat16)
    grad_down = jnp.dot(hidden.T, out_grad, preferred_element_type=jnp.float32).astype(jnp.bfloat16)
    grad_hidden = jnp.dot(out_grad, w_down.T, preferred_element_type=jnp.float32)
    sigmoid_gate = jax.nn.sigmoid(gate)
    gate_delta = (inverse[:, None] * grad_hidden * up_all * sigmoid_gate * (1.0 + gate * (1.0 - sigmoid_gate))).astype(jnp.bfloat16)
    up_delta = (inverse[:, None] * grad_hidden * gate * sigmoid_gate).astype(jnp.bfloat16)
    grad_gate = jnp.dot(scaled.T, gate_delta, preferred_element_type=jnp.float32).astype(jnp.bfloat16)
    grad_up = jnp.dot(scaled.T, up_delta, preferred_element_type=jnp.float32).astype(jnp.bfloat16)
    return (layer_out, grad_gate, grad_up, grad_down)
```

```python
import jax
import jax.numpy as jnp
from jax import lax
from jax.sharding import PartitionSpec as P

D = 8192


epsilon = 1e-05


def rank_in_block(shard_blocks):
    size = shard_blocks.shape[1]
    same = shard_blocks[:, :, None] == shard_blocks[:, None, :]
    earlier = jnp.arange(size)[None, :, None] > jnp.arange(size)[None, None, :]
    return jnp.sum((same & earlier).astype(jnp.int32), axis=2)


def shards(
    store_rows, source_shard, source_row, state_len, visits, gain, w_gate, w_up, w_down, upstream
):
    count_dp = lax.axis_size("dp")
    count_mp = lax.axis_size("mp")
    index_dp = lax.axis_index("dp")
    index_mp = lax.axis_index("mp")
    total_rows = source_shard.shape[0]
    block_rows = total_rows // count_dp
    share_rows = total_rows // count_mp
    pair_cap = max(block_rows // 8, 1)
    width = store_rows.shape[1]
    half = width // 2
    layers = count_dp // 4
    share_first = index_mp * share_rows

    def across(value, mask):
        return lax.ppermute(value, "dp", [(i, i ^ mask) for i in range(count_dp)])

    def along(value, step):
        return lax.ppermute(
            value, "dp", [(i, (i + 4 * step) % count_dp) for i in range(count_dp)]
        )

    def scatter_sum(value):
        if count_mp != 2:
            return lax.psum_scatter(value, "mp", scatter_dimension=0, tiled=True).astype(
                jnp.float32
            )
        other = lax.dynamic_slice_in_dim(value, share_rows - share_first, share_rows, 0)
        other = lax.ppermute(other.astype(jnp.bfloat16), "mp", [(0, 1), (1, 0)])
        own = lax.dynamic_slice_in_dim(value, share_first, share_rows, 0)
        return own.astype(jnp.float32) + other.astype(jnp.float32)

    def join(value):
        if count_mp != 2:
            return lax.all_gather(value, "mp", axis=0, tiled=True)
        other = lax.ppermute(value, "mp", [(0, 1), (1, 0)])
        first = index_mp == 0
        return jnp.concatenate(
            [jnp.where(first, value, other), jnp.where(first, other, value)], axis=0
        )

    shard_blocks = source_shard.reshape(count_dp, block_rows)
    row_blocks = source_row.reshape(count_dp, block_rows)
    ranks = rank_in_block(shard_blocks)
    slots = jnp.arange(pair_cap, dtype=jnp.int32)
    given = (shard_blocks == index_dp)[:, None, :] & (ranks[:, None, :] == slots[None, :, None])
    chosen = jnp.sum(jnp.where(given, row_blocks[:, None, :] + 1, 0), axis=2).reshape(-1) - 1
    pick = (chosen[:, None] == jnp.arange(store_rows.shape[0])[None, :]).astype(jnp.bfloat16)
    outgoing = jnp.dot(pick, store_rows, preferred_element_type=jnp.float32).astype(jnp.bfloat16)
    arrived = lax.all_to_all(
        outgoing.reshape(count_dp, pair_cap, width), "dp", 0, 0, tiled=True
    ).reshape(count_dp * pair_cap, width)
    own_slot = (
        lax.dynamic_index_in_dim(shard_blocks, index_dp, 0, False) * pair_cap
        + lax.dynamic_index_in_dim(ranks, index_dp, 0, False)
    )
    place = (own_slot[:, None] == jnp.arange(count_dp * pair_cap)[None, :]).astype(jnp.bfloat16)
    own_rows = jnp.dot(place, arrived, preferred_element_type=jnp.float32).astype(jnp.bfloat16)
    own_float = own_rows.astype(jnp.float32)
    squares = jnp.sum(own_float * own_float, axis=1)
    squares_all = lax.all_gather(squares, ("dp", "mp"), axis=0, tiled=False)
    square_total = jnp.sum(squares_all.reshape(count_dp, count_mp, block_rows), axis=1)
    own_scaled = (own_float * gain.astype(jnp.float32)[None, :]).astype(jnp.bfloat16)

    near, over_y, over_x, over_xy = [], [], [], []
    for step in range(layers):
        block = own_scaled if step == 0 else along(own_scaled, step)
        block_y = across(block, 2)
        block_x = across(block, 1)
        block_xy = jnp.concatenate(
            [across(block_y[:, :half], 1), across(block_x[:, half:], 2)], axis=1
        )
        near.append(block)
        over_y.append(block_y)
        over_x.append(block_x)
        over_xy.append(block_xy)
    scaled = jnp.concatenate(near + over_y + over_x + over_xy, axis=0)
    order = []
    for mask in (0, 2, 1, 3):
        for step in range(layers):
            order.append(lax.rem(index_dp + 4 * (layers - step), count_dp) ^ mask)
    inverse = lax.rsqrt(square_total / D + epsilon)[jnp.stack(order)].reshape(total_rows)

    row_ids = jnp.arange(total_rows, dtype=jnp.int32)
    ends = jnp.cumsum(state_len)
    starts = ends - state_len
    member = ((row_ids[:, None] >= starts[None, :]) & (row_ids[:, None] < ends[None, :])).astype(
        jnp.float32
    )
    importance = jnp.log1p(visits.astype(jnp.float32))
    per_state = total_rows * importance / (state_len.astype(jnp.float32) * jnp.sum(importance))
    row_weight = jnp.sum(member * per_state[None, :], axis=1)
    weighted = (upstream.astype(jnp.float32) * row_weight[:, None]).astype(jnp.bfloat16)
    out_grad = jnp.concatenate(
        [lax.dynamic_slice_in_dim(weighted, b * block_rows, block_rows, 0) for b in order], axis=0
    )
    grad_hidden = scatter_sum(
        lax.dot_general(
            out_grad, w_down, (((1,), (1,)), ((), ())), preferred_element_type=jnp.float32
        ).astype(jnp.bfloat16)
    )

    inverse_share = lax.dynamic_slice_in_dim(inverse, share_first, share_rows, 0)
    gate_share = inverse_share[:, None] * scatter_sum(
        jnp.dot(scaled, w_gate, preferred_element_type=jnp.float32)
    )
    up_share = inverse_share[:, None] * scatter_sum(
        jnp.dot(scaled, w_up, preferred_element_type=jnp.float32)
    )
    sigmoid_gate = jax.nn.sigmoid(gate_share)
    hidden_all = join((gate_share * sigmoid_gate * up_share).astype(jnp.bfloat16))

    middle = total_rows // 2
    far_part = jnp.dot(
        hidden_all[middle:], w_down, preferred_element_type=jnp.float32
    ).astype(jnp.bfloat16)
    near_part = jnp.dot(
        hidden_all[:middle], w_down, preferred_element_type=jnp.float32
    ).astype(jnp.bfloat16)
    group = middle // 2
    from_x = across(far_part[group:, :half], 1).astype(jnp.float32)
    from_y = across(far_part[group:, half:], 2).astype(jnp.float32)
    part_x = far_part[:group].astype(jnp.float32)
    part_x = jnp.concatenate([part_x[:, :half], part_x[:, half:] + from_y], axis=1)
    part_y = near_part[group:].astype(jnp.float32)
    part_y = jnp.concatenate([part_y[:, :half] + from_x, part_y[:, half:]], axis=1)
    part_x = part_x.astype(jnp.bfloat16)
    part_y = part_y.astype(jnp.bfloat16)
    down_block = jnp.zeros((block_rows, width), jnp.float32)
    for step in list(range(1, layers)) + [0]:
        rows = slice(step * block_rows, (step + 1) * block_rows)
        summed = (
            near_part[rows].astype(jnp.float32)
            + across(part_x[rows], 1).astype(jnp.float32)
            + across(part_y[rows], 2).astype(jnp.float32)
        )
        if step > 0:
            summed = along(summed.astype(jnp.bfloat16), layers - step).astype(jnp.float32)
        down_block = down_block + summed
    layer_out = (own_float + down_block).astype(jnp.bfloat16)

    grad_down = lax.dot_general(
        hidden_all, out_grad, (((0,), (0,)), ((), ())), preferred_element_type=jnp.float32
    ).astype(jnp.bfloat16)
    gate_delta = (
        inverse_share[:, None]
        * grad_hidden
        * up_share
        * sigmoid_gate
        * (1.0 + gate_share * (1.0 - sigmoid_gate))
    ).astype(jnp.bfloat16)
    up_delta = (inverse_share[:, None] * grad_hidden * gate_share * sigmoid_gate).astype(
        jnp.bfloat16
    )
    grad_gate = lax.dot_general(
        scaled, join(gate_delta), (((0,), (0,)), ((), ())), preferred_element_type=jnp.float32
    ).astype(jnp.bfloat16)
    grad_up = lax.dot_general(
        scaled, join(up_delta), (((0,), (0,)), ((), ())), preferred_element_type=jnp.float32
    ).astype(jnp.bfloat16)
    return (layer_out, grad_gate, grad_up, grad_down)


def solution(mesh):
    in_specs = (
        P("dp", "mp"),
        P(),
        P(),
        P(),
        P(),
        P("mp"),
        P("mp", "dp"),
        P("mp", "dp"),
        P("dp", "mp"),
        P(None, "mp"),
    )
    out_specs = (P("dp", "mp"), P("mp", "dp"), P("mp", "dp"), P("dp", "mp"))
    return jax.shard_map(shards, mesh=mesh, in_specs=in_specs, out_specs=out_specs, check_vma=False)
```

```python
import jax
import jax.numpy as jnp
from jax import lax
from jax.sharding import PartitionSpec as P

D = 8192


epsilon = 1e-05


def rank_in_block(shard_blocks):
    size = shard_blocks.shape[1]
    same = shard_blocks[:, :, None] == shard_blocks[:, None, :]
    earlier = jnp.arange(size)[None, :, None] > jnp.arange(size)[None, None, :]
    return jnp.sum((same & earlier).astype(jnp.int32), axis=2)


def shards(
    store_rows, source_shard, source_row, state_len, visits, gain, w_gate, w_up, w_down, upstream
):
    count_dp = lax.axis_size("dp")
    count_mp = lax.axis_size("mp")
    index_dp = lax.axis_index("dp")
    index_mp = lax.axis_index("mp")
    total_rows = source_shard.shape[0]
    block_rows = total_rows // count_dp
    share_rows = total_rows // count_mp
    pair_cap = max(block_rows // 8, 1)
    width = store_rows.shape[1]
    layers = count_dp // 4
    share_first = index_mp * share_rows

    def across(value, mask):
        return lax.ppermute(value, "dp", [(i, i ^ mask) for i in range(count_dp)])

    def along(value, step):
        return lax.ppermute(
            value, "dp", [(i, (i + 4 * step) % count_dp) for i in range(count_dp)]
        )

    def scatter_sum(value):
        if count_mp != 2:
            return lax.psum_scatter(value, "mp", scatter_dimension=0, tiled=True).astype(
                jnp.float32
            )
        other = lax.dynamic_slice_in_dim(value, share_rows - share_first, share_rows, 0)
        other = lax.ppermute(other.astype(jnp.bfloat16), "mp", [(0, 1), (1, 0)])
        own = lax.dynamic_slice_in_dim(value, share_first, share_rows, 0)
        return own.astype(jnp.float32) + other.astype(jnp.float32)

    def join(value):
        if count_mp != 2:
            return lax.all_gather(value, "mp", axis=0, tiled=True)
        other = lax.ppermute(value, "mp", [(0, 1), (1, 0)])
        first = index_mp == 0
        return jnp.concatenate(
            [jnp.where(first, value, other), jnp.where(first, other, value)], axis=0
        )

    shard_blocks = source_shard.reshape(count_dp, block_rows)
    row_blocks = source_row.reshape(count_dp, block_rows)
    ranks = rank_in_block(shard_blocks)
    slots = jnp.arange(pair_cap, dtype=jnp.int32)
    given = (shard_blocks == index_dp)[:, None, :] & (ranks[:, None, :] == slots[None, :, None])
    chosen = jnp.sum(jnp.where(given, row_blocks[:, None, :] + 1, 0), axis=2).reshape(-1) - 1
    pick = (chosen[:, None] == jnp.arange(store_rows.shape[0])[None, :]).astype(jnp.bfloat16)
    outgoing = jnp.dot(pick, store_rows, preferred_element_type=jnp.float32).astype(jnp.bfloat16)
    arrived = lax.all_to_all(
        outgoing.reshape(count_dp, pair_cap, width), "dp", 0, 0, tiled=True
    ).reshape(count_dp * pair_cap, width)
    own_slot = (
        lax.dynamic_index_in_dim(shard_blocks, index_dp, 0, False) * pair_cap
        + lax.dynamic_index_in_dim(ranks, index_dp, 0, False)
    )
    place = (own_slot[:, None] == jnp.arange(count_dp * pair_cap)[None, :]).astype(jnp.bfloat16)
    own_rows = jnp.dot(place, arrived, preferred_element_type=jnp.float32).astype(jnp.bfloat16)
    own_float = own_rows.astype(jnp.float32)
    squares = jnp.sum(own_float * own_float, axis=1)
    squares = jnp.concatenate(
        [squares] + [along(squares, step) for step in range(1, layers)], axis=0
    )
    squares = jnp.concatenate([squares, across(squares, 2)], axis=0)
    squares = jnp.concatenate([squares, across(squares, 1)], axis=0)
    if count_mp == 2:
        square_total = squares + lax.ppermute(squares, "mp", [(0, 1), (1, 0)])
    else:
        square_total = lax.psum(squares, "mp")
    own_scaled = (own_float * gain.astype(jnp.float32)[None, :]).astype(jnp.bfloat16)

    near, over_y, over_x, over_xy = [], [], [], []
    for step in range(layers):
        block = own_scaled if step == 0 else along(own_scaled, step)
        block_y = across(block, 2)
        block_x = across(block, 1)
        block_xy = across(block_y, 1) if step % 2 == 0 else across(block_x, 2)
        near.append(block)
        over_y.append(block_y)
        over_x.append(block_x)
        over_xy.append(block_xy)
    scaled = jnp.concatenate(near + over_y + over_x + over_xy, axis=0)
    scaled, square_total = lax.optimization_barrier((scaled, square_total))
    order = []
    for mask in (0, 2, 1, 3):
        for step in range(layers):
            order.append(lax.rem(index_dp + 4 * (layers - step), count_dp) ^ mask)
    inverse = lax.rsqrt(square_total / D + epsilon)

    row_ids = jnp.arange(total_rows, dtype=jnp.int32)
    ends = jnp.cumsum(state_len)
    starts = ends - state_len
    member = ((row_ids[:, None] >= starts[None, :]) & (row_ids[:, None] < ends[None, :])).astype(
        jnp.float32
    )
    importance = jnp.log1p(visits.astype(jnp.float32))
    per_state = total_rows * importance / (state_len.astype(jnp.float32) * jnp.sum(importance))
    row_weight = jnp.sum(member * per_state[None, :], axis=1)
    weighted = (upstream.astype(jnp.float32) * row_weight[:, None]).astype(jnp.bfloat16)
    out_grad = jnp.concatenate(
        [lax.dynamic_slice_in_dim(weighted, b * block_rows, block_rows, 0) for b in order], axis=0
    )
    grad_hidden = scatter_sum(
        lax.dot_general(
            out_grad, w_down, (((1,), (1,)), ((), ())), preferred_element_type=jnp.float32
        ).astype(jnp.bfloat16)
    )

    inverse_share = lax.dynamic_slice_in_dim(inverse, share_first, share_rows, 0)
    gate_share = inverse_share[:, None] * scatter_sum(
        jnp.dot(scaled, w_gate, preferred_element_type=jnp.float32)
    )
    up_share = inverse_share[:, None] * scatter_sum(
        jnp.dot(scaled, w_up, preferred_element_type=jnp.float32)
    )
    sigmoid_gate = jax.nn.sigmoid(gate_share)
    hidden_all = join((gate_share * sigmoid_gate * up_share).astype(jnp.bfloat16))

    middle = total_rows // 2
    far_part = jnp.dot(
        hidden_all[middle:], w_down, preferred_element_type=jnp.float32
    ).astype(jnp.bfloat16)
    near_part = jnp.dot(
        hidden_all[:middle], w_down, preferred_element_type=jnp.float32
    ).astype(jnp.bfloat16)
    group = middle // 2
    summed_x, summed_y = [], []
    parts_xy = [
        far_part[group + step * block_rows : group + (step + 1) * block_rows]
        for step in range(layers)
    ]
    parts_xy, near_part, hidden_late = lax.optimization_barrier((parts_xy, near_part, hidden_all))
    steps = list(range(1, layers)) + [0]
    for step in steps:
        rows = slice(step * block_rows, (step + 1) * block_rows)
        part_x = far_part[:group][rows]
        part_y = near_part[group:][rows]
        part_xy = parts_xy[step]
        if step % 2 == 0:
            part_y = part_y.astype(jnp.float32) + across(part_xy, 1).astype(jnp.float32)
        else:
            part_x = part_x.astype(jnp.float32) + across(part_xy, 2).astype(jnp.float32)
        summed_x.append(part_x.astype(jnp.bfloat16))
        summed_y.append(part_y.astype(jnp.bfloat16))
    summed_x, summed_y, scaled_late = lax.optimization_barrier((summed_x, summed_y, scaled))
    down_block = jnp.zeros((block_rows, width), jnp.float32)
    for step, part_x, part_y in zip(steps, summed_x, summed_y):
        rows = slice(step * block_rows, (step + 1) * block_rows)
        summed = (
            near_part[rows].astype(jnp.float32)
            + across(part_x, 1).astype(jnp.float32)
            + across(part_y, 2).astype(jnp.float32)
        )
        if step > 0:
            summed = along(summed.astype(jnp.bfloat16), layers - step).astype(jnp.float32)
        down_block = down_block + summed
    layer_out = (own_float + down_block).astype(jnp.bfloat16)

    grad_down = lax.dot_general(
        hidden_late, out_grad, (((0,), (0,)), ((), ())), preferred_element_type=jnp.float32
    ).astype(jnp.bfloat16)
    gate_delta = (
        inverse_share[:, None]
        * grad_hidden
        * up_share
        * sigmoid_gate
        * (1.0 + gate_share * (1.0 - sigmoid_gate))
    ).astype(jnp.bfloat16)
    up_delta = (inverse_share[:, None] * grad_hidden * gate_share * sigmoid_gate).astype(
        jnp.bfloat16
    )
    grad_gate = lax.dot_general(
        scaled_late, join(gate_delta), (((0,), (0,)), ((), ())), preferred_element_type=jnp.float32
    ).astype(jnp.bfloat16)
    grad_up = lax.dot_general(
        scaled_late, join(up_delta), (((0,), (0,)), ((), ())), preferred_element_type=jnp.float32
    ).astype(jnp.bfloat16)
    return (layer_out, grad_gate, grad_up, grad_down)


def solution(mesh):
    in_specs = (
        P("dp", "mp"),
        P(),
        P(),
        P(),
        P(),
        P("mp"),
        P("mp", "dp"),
        P("mp", "dp"),
        P("dp", "mp"),
        P(None, "mp"),
    )
    out_specs = (P("dp", "mp"), P("mp", "dp"), P("mp", "dp"), P("dp", "mp"))
    return jax.shard_map(shards, mesh=mesh, in_specs=in_specs, out_specs=out_specs, check_vma=False)
```
